256 devices in a mesh: group: 8 (over z), fsdp: 32 (over x, y, core).
Axes of the slice: x: 4, y: 4, z: 8, core: 2. Of those that a mesh axis runs over, the one named last changes fastest.
Arguments:
- grad_out: bfloat16 [16384, 4096], P(('group', 'fsdp')), may hold values from -6 to 6
- expert_ids: int32 [16384, 8], P(('group', 'fsdp')), may hold values from 0 to 127, all different within a row; in each aligned block of 64 rows (0 to 63, 64 to 127, ...) at most 5 rows name the same one
- gates: bfloat16 [16384, 8], P(('group', 'fsdp')), may hold values from 0.019897461 to 0.5
- hidden_saved: bfloat16 [256, 256, 5, 384], P(('group', 'fsdp')), may hold values from -0.59765625 to 0.59765625
- w_down: bfloat16 [256, 768, 2048], P(('group', 'fsdp')), may hold values from -0.21875 to 0.21875
Outputs:
- d_gate: float32 [16384, 8], P(('group', 'fsdp'))
- d_hidden: bfloat16 [256, 256, 5, 384], P(('group', 'fsdp'))
- d_weight: bfloat16 [256, 768, 2048], P(('group', 'fsdp'))
The draws below stay inside these ranges and needn't reach their ends.
Inputs may be any that keep to these rules, and one draw needn't show every extreme that they name: `expert_ids`: each row names 8 different experts; among the rows of one device no expert is named more than 5 times, and on some device some expert is named exactly 5 times.
All inputs are finite; a program needn't handle non-finite values.
Results may differ from the reference program's by a relative error of at most 0.0049.
Values may be sent and summed in bfloat16 or wider, within the bound.
A program may use at most 128 MiB of HBM per device.

```python
import math
import jax
import jax.numpy as jnp
import numpy as np
from jax import lax

D = 4096
TOP = 8
H = 768
TOK_DEV = 64
EXPERTS = 128
TOKENS = 16384
CAP = 5
N_GROUP = 8
N_FSDP = 32


def level_of(key, shape, split, low, high):
    loudness = 1.0
    for dim, shards_of in split:
        draws = jax.random.uniform(jax.random.fold_in(jax.random.fold_in(key, 6), dim), (shards_of,), jnp.float32, low / len(split), high / len(split))
        loudness = loudness * jnp.repeat(jnp.exp(draws), shape[dim] // shards_of).reshape((-1,) + (1,) * (len(shape) - 1 - dim))
    return loudness


def assign_block(key, own, number, rows, number_of, top, bound, slope):
    sequence = jax.random.permutation(key, number_of)
    packed, ordinary = shares(number_of, rows * top, bound, slope, True), shares(number_of, rows * top, bound, slope, False)
    places = jnp.arange(number_of)

    def named(lengths, turn):
        used = int((lengths > 0).sum())
        fixed = max(1, used // 4)
        shifted = fixed + (places - fixed + turn * (used - fixed)) % max(1, number_of - fixed)
        return jnp.zeros((number_of,), jnp.int32).at[sequence[jnp.where(places < fixed, places, shifted)]].set(jnp.asarray(lengths, jnp.int32))

    lengths = jnp.where(number % 4 == 0, named(packed, number // 4), named(ordinary, number - number // 4 - 1))
    mixed = jax.random.permutation(jax.random.fold_in(own, 3), number_of)
    source_of, taker = mixed[0:number_of // 2 * 2:2], mixed[1:number_of // 2 * 2:2]
    slack = jnp.minimum(lengths[source_of] - 1, bound - lengths[taker]) // 2
    slack = jnp.where((source_of == sequence[0]) | (taker == sequence[0]) | (lengths[taker] == 0), 0, jnp.maximum(slack, 0))
    shifted = jax.random.randint(jax.random.fold_in(own, 4), (number_of // 2,), 0, 1 << 20) % (slack + 1)
    lengths = lengths.at[source_of].add(-shifted).at[taker].add(shifted)
    members = jnp.searchsorted(jnp.cumsum(lengths), jnp.arange(rows * top), side="right").astype(jnp.int32)
    table = members.reshape(top, rows).T
    table = table[jax.random.permutation(jax.random.fold_in(own, 1), rows)]
    turn = jax.random.randint(jax.random.fold_in(own, 2), (rows, 1), 0, top)
    return jnp.take_along_axis(table, (jnp.arange(top)[None, :] + turn) % top, axis=1)


def shares(count, total, most, slope, full):
    weights = [(1 << 20) // math.isqrt(rank ** slope) + 1 for rank in range(1, count + 1)]
    largest = most if full else min(most, max(-(-total // count), total * weights[0] // sum(weights)))
    least = 1 if total - largest >= count - 1 else 0
    holding, spare = [largest] + [least] * (count - 1), total - largest - least * (count - 1)
    while spare > 0:
        candidates = [i for i in range(1, count) if holding[i] < largest] or [i for i in range(1, count) if holding[i] < most]
        whole, left = sum([weights[i] for i in candidates]), spare
        for i in candidates:
            addition = min(most - holding[i], max(1, left * weights[i] // whole), spare)
            holding[i] = holding[i] + addition
            spare = spare - addition
    return np.array(holding)


def noise(key, dims, spread, reach, cuts=(), kind=jnp.bfloat16):
    factor_of = level_of(key, dims, cuts, -0.22, 0.18) if cuts else 1.0
    drawn = jax.random.normal(key, dims, jnp.float32) * spread * factor_of
    return jnp.minimum(jnp.maximum(drawn, -reach), reach).astype(kind)


def setup_inputs(seed: int = 0) -> dict:
    key_of = jax.random.split(jax.random.key(seed), 6)
    grad_out = noise(key_of[0], (TOKENS, D), 1.0, 6.0, ((0, 256),))
    expert_ids_keys = jax.random.split(jax.random.fold_in(key_of[1], 1), TOKENS // TOK_DEV)
    expert_ids_turns = jax.random.permutation(jax.random.fold_in(key_of[1], 3), TOKENS // TOK_DEV)
    expert_ids = jax.vmap(lambda own, number: assign_block(jax.random.fold_in(key_of[1], 2), own, number, TOK_DEV, EXPERTS, TOP, CAP, 1))(expert_ids_keys, expert_ids_turns).reshape((TOKENS, TOP))
    gates = jnp.clip(jnp.exp(math.log(0.5) - 3.224016 * jax.random.uniform(key_of[2], (TOKENS, TOP), jnp.float32) ** level_of(key_of[2], (TOKENS, TOP), ((0, 256),), -0.2, 0.2)), 0.019897461, 0.5).astype(jnp.bfloat16)
    hidden_saved = noise(key_of[3], (N_GROUP * N_FSDP, N_GROUP * N_FSDP, CAP, H // 2), 0.1, 0.59765625, ((0, 256),))
    w_down = noise(key_of[4], (N_GROUP * N_FSDP, H, D // 2), H ** -0.5, 0.21875, ((0, 256),))
    return {"grad_out": grad_out, "expert_ids": expert_ids, "gates": gates, "hidden_saved": hidden_saved, "w_down": w_down}


def block_ranks(labels):
    onehot = (labels[:, None] == jnp.arange(EXPERTS, dtype=jnp.int32)[None, :]).astype(jnp.int32)
    before = jnp.cumsum(onehot, axis=0) - onehot
    return jnp.sum(before * onehot, axis=1).astype(jnp.int32)


def reference(grad_out, expert_ids, gates, hidden_saved, w_down):
    devices = N_GROUP * N_FSDP
    width = TOK_DEV * TOP
    labels = expert_ids.reshape(devices, width).astype(jnp.int32)
    ranking = lax.map(block_ranks, labels)
    source = jnp.broadcast_to(jnp.arange(devices, dtype=jnp.int32)[:, None], (devices, width))
    position = ((labels * devices + source) * CAP + ranking).reshape(-1).astype(jnp.int32)
    entries = jnp.arange(devices * width, dtype=jnp.int32)
    lookup = jnp.full((EXPERTS * devices * CAP,), -1, jnp.int32).at[position].set(entries)
    lookup = lookup.reshape(EXPERTS, devices * CAP)
    gate_flat = gates.reshape(-1)
    saved = hidden_saved.reshape(EXPERTS, 2, devices * CAP, H // 2)
    weights = w_down.reshape(EXPERTS, 2, H, D // 2)

    def per_expert(pieces):
        slot_ids, halves, matrix_halves = pieces
        active = slot_ids >= 0
        chosen = jnp.where(active, slot_ids, 0)
        row_data = jnp.where(active[:, None], grad_out[chosen // TOP], jnp.zeros((), grad_out.dtype))
        weighting = jnp.where(active, gate_flat[chosen].astype(jnp.float32), jnp.zeros((), jnp.float32))[:, None]
        hidden = jnp.concatenate([halves[0], halves[1]], axis=1).astype(jnp.float32)
        matrix = jnp.concatenate([matrix_halves[0], matrix_halves[1]], axis=1)
        product = lax.dot_general(row_data, matrix, (((1,), (1,)), ((), ())), preferred_element_type=jnp.float32)
        gate_grad = jnp.sum(product * hidden, axis=1)
        hidden_grad = (weighting * product).astype(jnp.bfloat16)
        scaled = (weighting * hidden).astype(jnp.bfloat16)
        weight_grad = lax.dot_general(scaled, row_data, (((0,), (0,)), ((), ())), preferred_element_type=jnp.float32).astype(jnp.bfloat16)
        return gate_grad, hidden_grad, weight_grad

    gate_grad, hidden_grad, weight_grad = lax.map(per_expert, (lookup, saved, weights))
    d_gate = gate_grad.reshape(-1)[position].reshape(TOKENS, TOP)
    d_hidden = hidden_grad.reshape(EXPERTS, devices * CAP, 2, H // 2).transpose(0, 2, 1, 3).reshape(devices, devices, CAP, H // 2)
    d_weight = weight_grad.reshape(EXPERTS, H, 2, D // 2).transpose(0, 2, 1, 3).reshape(devices, H, D // 2)
    return d_gate, d_hidden, d_weight
```

```python
import jax
import jax.numpy as jnp
from jax import lax
from jax.experimental import pallas as pl
from jax.experimental.pallas import tpu as pltpu
from jax.sharding import PartitionSpec as P

MESH = pl.DeviceIdType.MESH
F32 = jnp.float32
BF16 = jnp.bfloat16

NZ, NX, NY = 8, 4, 4
NP = NX * NY
TOK, TOP = 64, 8
CAP = 5
SRC = 2 * NZ
ROWS = CAP * SRC
HALF_D, H, HALF_H = 2048, 768, 384
EXPERTS = NZ * NP
DEAD = -1000.0

WIDTHS = (256,) * 8
STARTS = tuple(sum(WIDTHS[:i]) for i in range(len(WIDTHS)))
K = len(WIDTHS)


def iota(shape, dim):
    return lax.broadcasted_iota(jnp.int32, shape, dim)


def nt(a, b):
    return lax.dot_general(a, b, (((1,), (1,)), ((), ())), preferred_element_type=F32)


def nn(a, b):
    return lax.dot_general(a, b, (((1,), (0,)), ((), ())), preferred_element_type=F32)


def wait_for(ref, sem):
    pltpu.make_async_copy(ref, ref, sem).wait()


def kernel(
    g_hbm, ids_ref, gates_ref, h_hbm, w_hbm,
    dgate_ref, dh_hbm, dw_hbm,
    tok, send, recv, pick, w_v, uacc, h_raw, h_all, scaled_t, dw_v, uex, dh_v, gate_col,
    idx_mine, idx_other, meta_s, meta_r, code, gate_g, gm_s, gm_r, gp_s, gp_r, g2_s, g2_r, look, zmask,
    sem_h, sem_w, sem_loc, swap_s, swap_r, idx_sem, hx_sem, meta_ss, meta_rs,
    z_s, z_r, xy_s, xy_r, gm_ss, gm_rs, ex_s, ex_r, gp_ss, gp_rs, g2_ss, g2_rs, dw_sem, dh_sem,
):
    z = lax.axis_index("group")
    f = lax.axis_index("fsdp")
    p = f // 2
    core = f % 2
    x = p // NY
    y = p % NY
    other = 1 - core

    def plane(i):
        dx, dy = i // NY, i % NY
        return ((x + dx) % NX) * NY + (y + dy) % NY

    sibling = (z, p * 2 + other)

    def remote(src, dst, ss, rs, dev):
        return pltpu.make_async_remote_copy(
            src_ref=src, dst_ref=dst, send_sem=ss, recv_sem=rs, device_id=dev, device_id_type=MESH
        )

    locals_ = []
    for k in range(K):
        cp = pltpu.make_async_copy(
            g_hbm.at[:, pl.ds(pl.multiple_of(core * HALF_D + STARTS[k], 128), WIDTHS[k])],
            tok.at[z, core, :, pl.ds(STARTS[k], WIDTHS[k])],
            sem_loc.at[k],
        )
        cp.start()
        locals_.append(cp)
    h_in = pltpu.make_async_copy(h_hbm, h_raw.at[core], sem_h)
    h_in.start()
    w_in = pltpu.make_async_copy(w_hbm, w_v, sem_w)
    w_in.start()

    barrier = pltpu.get_barrier_semaphore()
    partners = [sibling]
    for d in range(1, NZ):
        partners.append(((z + d) % NZ, f))
        partners.append(((z + d) % NZ, p * 2 + other))
    for i in range(1, NP):
        partners.append((z, plane(i) * 2 + core))
    for dev in partners:
        pl.semaphore_signal(barrier, 1, device_id=dev, device_id_type=MESH)
    pl.semaphore_wait(barrier, len(partners))

    swaps = []
    for k in range(K):
        cols = pl.ds(STARTS[k], WIDTHS[k])
        cp = remote(
            g_hbm.at[:, pl.ds(pl.multiple_of(other * HALF_D + STARTS[k], 128), WIDTHS[k])],
            tok.at[z, core, :, cols], swap_s.at[k], swap_r.at[k], sibling,
        )
        swaps.append(cp)
    swaps[0].start()

    lanes16 = iota((16, 128), 1)
    both = jnp.concatenate([ids_ref[...].astype(F32), gates_ref[...].astype(F32)], axis=0)
    twice = jnp.concatenate([both, both], axis=1)
    idx_mine[...] = jnp.where(lanes16 // TOK == core, twice, 0.0)
    idx_cp = remote(idx_mine, idx_other, idx_sem.at[0], idx_sem.at[1], sibling)
    idx_cp.start()
    for k in range(1, K):
        swaps[k].start()
    hx_cp = remote(h_hbm, h_raw.at[core], hx_sem.at[0], hx_sem.at[1], sibling)
    hx_cp.start()

    def ring(k, hop, way):
        sign = 1 if way == 0 else -1
        slot = (z - sign * (hop - 1) + 2 * NZ) % NZ
        ref = tok.at[slot, :, :, pl.ds(STARTS[k], WIDTHS[k])]
        return remote(ref, ref, z_s.at[k], z_r.at[way, hop - 1, k], ((z + sign + NZ) % NZ, f))

    def arrived(k, hop, way):
        sign = 1 if way == 0 else -1
        slot = (z - sign * hop + 2 * NZ) % NZ
        ref = tok.at[slot, :, :, pl.ds(STARTS[k], WIDTHS[k])]
        wait_for(ref, z_r.at[way, hop - 1, k])

    def hop1(k):
        locals_[k].wait()
        swaps[k].wait_recv()
        ring(k, 1, 0).start()
        ring(k, 1, 1).start()

    def hop23(k, hop):
        for way in (0, 1):
            arrived(k, hop - 1, way)
            ring(k, hop, way).start()

    def hop4(k):
        way = k % 2
        arrived(k, 3, way)
        ring(k, 4, way).start()

    def gathered(k):
        arrived(k, 3, 1 - k % 2)
        arrived(k, 4, k % 2)

    hop1(0)

    idx_cp.wait_recv()
    table = idx_mine[...] + idx_other[...]
    expert = iota((EXPERTS, 128), 0).astype(F32)
    named = jnp.zeros((EXPERTS, 128), F32)
    by_expert = jnp.zeros((EXPERTS, 128), F32)
    for k in range(TOP):
        hit = expert == table[k : k + 1]
        named = named + jnp.where(hit, 1.0, 0.0)
        by_expert = by_expert + jnp.where(hit, table[TOP + k : TOP + k + 1], 0.0)
    before = iota((128, 128), 0)
    after = iota((128, 128), 1)
    upper = jnp.where((before < after) & (before // TOK == after // TOK), 1.0, 0.0).astype(BF16)
    rank = nn(named.astype(BF16), upper)
    rank_or = jnp.where(named > 0, rank, DEAD).astype(BF16)
    meta_s[:, 0:16] = rank_or.reshape(NZ, NP, 128)
    meta_s[:, 16:32] = by_expert.astype(BF16).reshape(NZ, NP, 128)
    metas = []
    for d in range(1, NZ):
        to = (z + d) % NZ
        cp = remote(meta_s.at[to], meta_r.at[z], meta_ss.at[d - 1], meta_rs.at[d - 1], (to, f))
        cp.start()
        metas.append(cp)
    meta_r[z] = meta_s[z]

    hop1(1)
    hop23(0, 2)

    lane_l = iota((128, 128), 0)
    sub8 = iota((8, 128), 0)
    for k in range(TOP):
        ids_k = table[k : k + 1]
        rank_k = jnp.sum(jnp.where(expert == ids_k, rank, 0.0), axis=0, keepdims=True)
        ids_i = ids_k.astype(jnp.int32)
        place = (ids_i % NP) * CAP + rank_k.astype(jnp.int32)
        look[:, k * 128 : (k + 1) * 128] = jnp.where(lane_l == place, 1.0, 0.0).astype(BF16)
        zmask[:, k * 128 : (k + 1) * 128] = jnp.where(sub8 == ids_i // NP, 1.0, 0.0)

    hop1(2)
    hop23(1, 2)
    hop23(0, 3)

    for cp in metas:
        cp.wait_recv()
    for j in range(NZ):
        lane_src = (j * 128 + iota((NP, 128), 1)) // TOK
        code[:, j * 128 : (j + 1) * 128] = meta_r[j, 0:16].astype(F32) + 8.0 * lane_src.astype(F32)
        gate_g[:, j * 128 : (j + 1) * 128] = meta_r[j, 16:32]
    row = iota((ROWS, 1024), 0)
    target = (row // SRC + 8 * (row % SRC)).astype(F32)

    @pl.loop(0, NP)
    def _(e):
        chosen = jnp.where(code[pl.ds(e, 1), :] == target, 1.0, 0.0).astype(BF16)
        pick[e] = chosen
        gm = nt(gate_g[...], chosen)
        gm_s[e] = jnp.concatenate([gm, jnp.zeros((NP, 128 - ROWS), F32)], axis=1).astype(BF16)

    hop1(3)
    hop23(2, 2)
    hop23(1, 3)
    hop4(0)

    for i in range(1, NP):
        to = plane(i)
        remote(gm_s.at[to], gm_r.at[p], gm_ss, gm_rs, (z, to * 2 + core)).start()
    gm_r[p] = gm_s[p]

    def select(k):
        cols = pl.ds(STARTS[k], WIDTHS[k])
        w = WIDTHS[k]

        @pl.loop(0, NP // 4)
        def _(q):
            lhs = pick[pl.ds(q * 4, 4)].reshape(4 * ROWS, 1024)
            out = nn(lhs, tok[:, :, :, cols].reshape(1024, w))
            send[pl.ds(q * 4, 4), :, :, cols] = out.astype(BF16).reshape(4, CAP, SRC, w)

        for i in range(1, NP):
            to = plane(i)
            remote(
                send.at[to, :, :, cols], recv.at[:, p, :, cols], xy_s.at[k], xy_r.at[k],
                (z, to * 2 + core),
            ).start()
        recv[:, p, :, cols] = send[p, :, :, cols]

    r_i = iota((256, 256), 0)
    s_i = iota((256, 256), 1)
    perm = jnp.where(((r_i % 16) // 2) * 32 + (r_i // 16) * 2 + r_i % 2 == s_i, 1.0, 0.0).astype(BF16)
    back = jnp.where(((r_i % 32) // 2) * 16 + (r_i // 32) * 2 + r_i % 2 == s_i, 1.0, 0.0).astype(BF16)
    eye = jnp.where(r_i == s_i, 1.0, 0.0).astype(BF16)

    def hidden_task():
        h_in.wait()
        hx_cp.wait_recv()
        for j in range(2):
            for c in range(CAP):
                h_all[c, :, j * HALF_H : (j + 1) * HALF_H] = nn(perm, h_raw[j, c]).astype(BF16)

    def gate_task():
        wait_for(gm_r.at[pl.ds(0, NP - 1)], gm_rs)
        mine = jnp.where(iota((NP, NP, 128), 1) == p, gm_r[...].astype(F32), 0.0)
        gates = jnp.sum(mine, axis=1).astype(BF16)
        spread = jnp.where(iota((256, NP), 0) // SRC == iota((256, NP), 1), 1.0, 0.0).astype(BF16)
        wide = nn(spread, gates)
        lane = iota((256, 128), 1)
        src = iota((256, 128), 0) % SRC
        for c in range(CAP):
            col = jnp.sum(jnp.where(lane == c * SRC + src, wide, 0.0), axis=1, keepdims=True)
            gate_col[c] = jnp.broadcast_to(col, (256, 128))
            scaled = (col * h_all[c].astype(F32)).astype(BF16)
            for b in range(3):
                scaled_t[b * 256 : (b + 1) * 256, c * 256 : (c + 1) * 256] = nt(
                    eye, scaled[:, b * 256 : (b + 1) * 256]
                ).astype(BF16)

    def take_u(k):
        cols = pl.ds(STARTS[k], WIDTHS[k])
        w = WIDTHS[k]
        wait_for(recv.at[:, pl.ds(0, NP - 1), :, cols], xy_r.at[k])

        @pl.loop(0, CAP)
        def _(c):
            part = nt(recv[c, :, :, cols].reshape(256, w), w_v[:, cols])
            if k == 0:
                uacc[c] = part
            else:
                uacc[c] += part

    def take_w(k):
        cols = pl.ds(STARTS[k], WIDTHS[k])
        w = WIDTHS[k]

        @pl.loop(0, 3)
        def _(b):
            rows = pl.ds(pl.multiple_of(b * 256, 256), 256)
            out = nn(scaled_t[rows, :], recv[:, :, :, cols].reshape(5 * 256, w))
            dw_v[rows, cols] = out.astype(BF16)

        pltpu.make_async_copy(dw_v.at[:, cols], dw_hbm.at[:, cols], dw_sem.at[k]).start()

    for t in range(4, K + 6):
        if t < K:
            hop1(t)
        if t - 1 < K:
            hop23(t - 1, 2)
        if t - 2 < K:
            hop23(t - 2, 3)
        if t - 3 < K:
            hop4(t - 3)
        if t - 4 < K:
            gathered(t - 4)
            select(t - 4)
        if t == 4:
            hidden_task()
        if t == 5:
            gate_task()
            w_in.wait()
        if t >= 6:
            take_u(t - 6)
            if t - 6 < K - 1:
                take_w(t - 6)

    exs = []
    lane_t = iota((256, 128), 1)
    terms = jnp.zeros((256, 128), F32)
    for c in range(CAP):
        cp = remote(
            uacc.at[c, :, pl.ds(pl.multiple_of(other * HALF_H, 128), HALF_H)], uex.at[c],
            ex_s.at[c], ex_r.at[c], sibling,
        )
        cp.start()
        exs.append(cp)
    for c in range(CAP):
        part = jnp.sum(uacc[c] * h_all[c].astype(F32), axis=1, keepdims=True)
        terms = terms + jnp.where(lane_t == p * CAP + c, part, 0.0)
    gp_s[...] = terms.reshape(NP, SRC, 128)
    for i in range(1, NP):
        to = plane(i)
        remote(gp_s.at[to], gp_r.at[p], gp_ss, gp_rs, (z, to * 2 + core)).start()
    gp_r[p] = gp_s[p]

    take_w(K - 1)

    def finish_hidden(c):
        exs[c].wait_recv()
        u = uacc[c, :, pl.ds(pl.multiple_of(core * HALF_H, 128), HALF_H)] + uex[c]
        dh = (gate_col[c, :, 0:1] * u).astype(BF16)
        dh_v[c] = nn(back, dh).astype(BF16)
        pltpu.make_async_copy(dh_v.at[c], dh_hbm.at[c], dh_sem.at[c]).start()

    for c in range(CAP):
        finish_hidden(c)

    wait_for(gp_r.at[pl.ds(0, NP - 1)], gp_rs)
    total = jnp.sum(gp_r[...], axis=0)
    g2_s[...] = jnp.broadcast_to(total[:, None, :], (SRC, 8, 128))
    g2 = []
    for d in range(NZ):
        to = (z + d) % NZ
        for flip in (0, 1):
            if d == 0 and flip == 0:
                continue
            to_core = core if flip == 0 else other
            n = 2 * d + flip - 1
            cp = remote(
                g2_s.at[to * 2 + to_core], g2_r.at[core, z], g2_ss.at[n], g2_rs.at[n],
                (to, p * 2 + to_core),
            )
            cp.start()
            g2.append(cp)
    g2_r[core, z] = g2_s[z * 2 + core]
    for cp in g2:
        cp.wait_recv()
    summed = g2_r[0] + g2_r[1]
    zi = iota((NZ, 8, 128), 0)
    si = iota((NZ, 8, 128), 1)
    terms8 = jnp.sum(jnp.where(zi == si, summed, 0.0), axis=0)
    hi = terms8.astype(BF16)
    rest = terms8 - hi.astype(F32)
    mid = rest.astype(BF16)
    low = (rest - mid.astype(F32)).astype(BF16)
    for k in range(TOP):
        lk = look[:, k * 128 : (k + 1) * 128]
        got = nn(hi, lk) + nn(mid, lk) + nn(low, lk)
        line = jnp.sum(got * zmask[:, k * 128 : (k + 1) * 128], axis=0, keepdims=True)
        dgate_ref[k : k + 1, :] = jnp.where(core == 0, line[:, 0:TOK], line[:, TOK:])

    idx_cp.wait_send()
    hx_cp.wait_send()
    for cp in swaps + metas + exs + g2:
        cp.wait_send()
    for k in range(K):
        cols = pl.ds(STARTS[k], WIDTHS[k])
        wait_for(tok.at[pl.ds(0, NZ - 1), :, :, cols], z_s.at[k])
        wait_for(recv.at[:, pl.ds(0, NP - 1), :, cols], xy_s.at[k])
        pltpu.make_async_copy(dw_v.at[:, cols], dw_hbm.at[:, cols], dw_sem.at[k]).wait()
    for c in range(CAP):
        pltpu.make_async_copy(dh_v.at[c], dh_hbm.at[c], dh_sem.at[c]).wait()
    wait_for(gm_r.at[pl.ds(0, NP - 1)], gm_ss)
    wait_for(gp_r.at[pl.ds(0, NP - 1)], gp_ss)


def local(grad_out, expert_ids, gates, hidden_saved, w_down):
    dma = pltpu.SemaphoreType.DMA
    vm = pltpu.VMEM
    anywhere = pl.BlockSpec(memory_space=pl.ANY)
    in_vmem = pl.BlockSpec(memory_space=pltpu.VMEM)
    scratch = [
        vm((NZ, 2, TOK, HALF_D), BF16),
        vm((NP, CAP, SRC, HALF_D), BF16),
        vm((CAP, NP, SRC, HALF_D), BF16),
        vm((NP, ROWS, 1024), BF16),
        vm((H, HALF_D), BF16),
        vm((CAP, 256, H), F32),
        vm((2, CAP, 256, HALF_H), BF16),
        vm((CAP, 256, H), BF16),
        vm((H, CAP * 256), BF16),
        vm((H, HALF_D), BF16),
        vm((CAP, 256, HALF_H), F32),
        vm((CAP, 256, HALF_H), BF16),
        vm((CAP, 256, 128), F32),
        vm((16, 128), F32),
        vm((16, 128), F32),
        vm((NZ, 32, 128), BF16),
        vm((NZ, 32, 128), BF16),
        vm((NP, 1024), F32),
        vm((NP, 1024), BF16),
        vm((NP, NP, 128), BF16),
        vm((NP, NP, 128), BF16),
        vm((NP, SRC, 128), F32),
        vm((NP, SRC, 128), F32),
        vm((SRC, 8, 128), F32),
        vm((2, NZ, 8, 128), F32),
        vm((128, TOP * 128), BF16),
        vm((8, TOP * 128), F32),
        dma, dma, dma((K,)), dma((K,)), dma((K,)), dma((2,)), dma((2,)), dma((7,)), dma((7,)),
        dma((K,)), dma((2, 4, K)), dma((K,)), dma((K,)), dma, dma, dma((CAP,)), dma((CAP,)),
        dma, dma, dma((15,)), dma((15,)), dma((K,)), dma((CAP,)),
    ]
    d_gate, d_hidden, d_weight = pl.pallas_call(
        kernel,
        out_shape=(
            jax.ShapeDtypeStruct((TOP, TOK), F32),
            jax.ShapeDtypeStruct((CAP, 256, HALF_H), BF16),
            jax.ShapeDtypeStruct((H, HALF_D), BF16),
        ),
        in_specs=[anywhere, in_vmem, in_vmem, anywhere, anywhere],
        out_specs=(in_vmem, anywhere, anywhere),
        scratch_shapes=scratch,
        compiler_params=pltpu.CompilerParams(
            collective_id=0, has_side_effects=True, vmem_limit_bytes=56 * 2**20
        ),
        cost_estimate=pl.CostEstimate(
            flops=15 * 10**9, bytes_accessed=10 * 10**6, transcendentals=0
        ),
    )(grad_out, expert_ids.T, gates.T, jnp.transpose(hidden_saved[0], (1, 0, 2)), w_down[0])
    return d_gate.T, jnp.transpose(d_hidden, (1, 0, 2))[None], d_weight[None]


def solution(mesh):
    spec = P(("group", "fsdp"), None)
    in_specs = (
        spec,
        spec,
        spec,
        P(("group", "fsdp"), None, None, None),
        P(("group", "fsdp"), None, None),
    )
    out_specs = (spec, P(("group", "fsdp"), None, None, None), P(("group", "fsdp"), None, None))
    return jax.shard_map(local, mesh=mesh, in_specs=in_specs, out_specs=out_specs, check_vma=False)
```

```python
import jax
import jax.numpy as jnp
from jax import lax
from jax.experimental import pallas as pl
from jax.experimental.pallas import tpu as pltpu
from jax.sharding import PartitionSpec as P

MESH = pl.DeviceIdType.MESH
F32 = jnp.float32
BF16 = jnp.bfloat16

NZ, NX, NY = 8, 4, 4
NP = NX * NY
TOK, TOP = 64, 8
CAP = 5
SRC = 2 * NZ
ROWS = CAP * SRC
HALF_D, H, HALF_H = 2048, 768, 384
EXPERTS = NZ * NP
DEAD = -1000.0

WIDTHS = (256,) * 8
STARTS = tuple(sum(WIDTHS[:i]) for i in range(len(WIDTHS)))
K = len(WIDTHS)


def iota(shape, dim):
    return lax.broadcasted_iota(jnp.int32, shape, dim)


def nt(a, b):
    return lax.dot_general(a, b, (((1,), (1,)), ((), ())), preferred_element_type=F32)


def nn(a, b):
    return lax.dot_general(a, b, (((1,), (0,)), ((), ())), preferred_element_type=F32)


def wait_for(ref, sem):
    pltpu.make_async_copy(ref, ref, sem).wait()


def kernel(
    g_hbm, ids_ref, gates_ref, h_hbm, w_hbm,
    dgate_ref, dh_hbm, dw_hbm,
    tok, send, recv, pick, w_v, uacc, h_raw, h_all, scaled_t, dw_v, uex, dh_v, gate_col,
    idx_s, idx_r, code, gate_g, gm_s, gm_r, gp_s, gp_r, g2_s, g2_r, look, zmask,
    sem_h, sem_w, sem_loc, swap_s, swap_r, idx_ss, idx_rs, hx_sem, first_s, first_r,
    z_s, z_r, xy_s, xy_r, gm_ss, gm_rs, ex_s, ex_r, gp_ss, gp_rs, g2_ss, g2_rs, dw_sem, dh_sem,
):
    z = lax.axis_index("group")
    f = lax.axis_index("fsdp")
    p = f // 2
    core = f % 2
    x = p // NY
    y = p % NY
    other = 1 - core

    def plane(i):
        dx, dy = i // NY, i % NY
        return ((x + dx) % NX) * NY + (y + dy) % NY

    sibling = (z, p * 2 + other)

    def remote(src, dst, ss, rs, dev):
        return pltpu.make_async_remote_copy(
            src_ref=src, dst_ref=dst, send_sem=ss, recv_sem=rs, device_id=dev, device_id_type=MESH
        )

    locals_ = []
    for k in range(K):
        cp = pltpu.make_async_copy(
            g_hbm.at[:, pl.ds(pl.multiple_of(core * HALF_D + STARTS[k], 128), WIDTHS[k])],
            tok.at[z, core, :, pl.ds(STARTS[k], WIDTHS[k])],
            sem_loc.at[k],
        )
        cp.start()
        locals_.append(cp)
    h_in = pltpu.make_async_copy(h_hbm, h_raw.at[core], sem_h)
    h_in.start()
    w_in = pltpu.make_async_copy(w_hbm, w_v, sem_w)
    w_in.start()

    barrier = pltpu.get_barrier_semaphore()
    partners = [sibling]
    for d in range(1, NZ):
        partners.append(((z + d) % NZ, f))
        partners.append(((z + d) % NZ, p * 2 + other))
    for i in range(1, NP):
        partners.append((z, plane(i) * 2 + core))
    for dev in partners:
        pl.semaphore_signal(barrier, 1, device_id=dev, device_id_type=MESH)
    pl.semaphore_wait(barrier, len(partners))

    line = [sibling]
    for d in range(1, NZ):
        line.append(((z + d) % NZ, f))
        line.append(((z + d) % NZ, p * 2 + other))

    lanes16 = iota((16, 128), 1)
    both = jnp.concatenate([ids_ref[...].astype(F32), gates_ref[...].astype(F32)], axis=0)
    twice = jnp.concatenate([both, both], axis=1)
    idx_s[...] = jnp.where(lanes16 // TOK == core, twice, 0.0)
    idxs = []
    for i, dev in enumerate(line):
        cp = remote(idx_s, idx_r.at[z, core], idx_ss.at[i], idx_rs.at[i], dev)
        cp.start()
        idxs.append(cp)

    first_cols = pl.ds(0, WIDTHS[0])
    for d in range(1, NZ):
        for to_core in (0, 1):
            remote(
                g_hbm.at[:, pl.ds(to_core * HALF_D, WIDTHS[0])],
                tok.at[z, core, :, first_cols], first_s, first_r,
                ((z + d) % NZ, p * 2 + to_core),
            ).start()

    swaps = []
    for k in range(K):
        cols = pl.ds(STARTS[k], WIDTHS[k])
        cp = remote(
            g_hbm.at[:, pl.ds(pl.multiple_of(other * HALF_D + STARTS[k], 128), WIDTHS[k])],
            tok.at[z, core, :, cols], swap_s.at[k], swap_r.at[k], sibling,
        )
        cp.start()
        swaps.append(cp)
    hx_cp = remote(h_hbm, h_raw.at[core], hx_sem.at[0], hx_sem.at[1], sibling)
    hx_cp.start()
    idx_r[z, core] = idx_s[...]

    def ring(k, hop, way):
        sign = 1 if way == 0 else -1
        slot = (z - sign * (hop - 1) + 2 * NZ) % NZ
        ref = tok.at[slot, :, :, pl.ds(STARTS[k], WIDTHS[k])]
        return remote(ref, ref, z_s.at[k], z_r.at[way, hop - 1, k], ((z + sign + NZ) % NZ, f))

    def arrived(k, hop, way):
        sign = 1 if way == 0 else -1
        slot = (z - sign * hop + 2 * NZ) % NZ
        ref = tok.at[slot, :, :, pl.ds(STARTS[k], WIDTHS[k])]
        wait_for(ref, z_r.at[way, hop - 1, k])

    def hop1(k):
        locals_[k].wait()
        swaps[k].wait_recv()
        ring(k, 1, 0).start()
        ring(k, 1, 1).start()

    def hop23(k, hop):
        for way in (0, 1):
            arrived(k, hop - 1, way)
            ring(k, hop, way).start()

    def hop4(k):
        way = k % 2
        arrived(k, 3, way)
        ring(k, 4, way).start()

    def gathered(k):
        arrived(k, 3, 1 - k % 2)
        arrived(k, 4, k % 2)

    for k in range(1, 5):
        hop1(k)

    for cp in idxs:
        cp.wait_recv()
    before = iota((128, 128), 0)
    after = iota((128, 128), 1)
    upper = jnp.where((before < after) & (before // TOK == after // TOK), 1.0, 0.0).astype(BF16)
    plane_expert = (z * NP + iota((NP, 128), 0)).astype(F32)
    for j in range(NZ):
        tab = idx_r[j, 0] + idx_r[j, 1]
        named = jnp.zeros((NP, 128), F32)
        by_expert = jnp.zeros((NP, 128), F32)
        for k in range(TOP):
            hit = plane_expert == tab[k : k + 1]
            named = named + jnp.where(hit, 1.0, 0.0)
            by_expert = by_expert + jnp.where(hit, tab[TOP + k : TOP + k + 1], 0.0)
        rank = nn(named.astype(BF16), upper)
        lane_src = (j * 128 + iota((NP, 128), 1)) // TOK
        coded = jnp.where(named > 0, rank + 8.0 * lane_src.astype(F32), DEAD)
        code[:, j * 128 : (j + 1) * 128] = coded
        gate_g[:, j * 128 : (j + 1) * 128] = by_expert.astype(BF16)
    row = iota((ROWS, 1024), 0)
    target = (row // SRC + 8 * (row % SRC)).astype(F32)

    @pl.loop(0, NP)
    def _(e):
        pick[e] = jnp.where(code[pl.ds(e, 1), :] == target, 1.0, 0.0).astype(BF16)

    def look_task():
        table = idx_r[z, 0] + idx_r[z, 1]
        expert = iota((EXPERTS, 128), 0).astype(F32)
        named = jnp.zeros((EXPERTS, 128), F32)
        for k in range(TOP):
            named = named + jnp.where(expert == table[k : k + 1], 1.0, 0.0)
        rank = nn(named.astype(BF16), upper)
        lane_l = iota((128, 128), 0)
        sub8 = iota((8, 128), 0)
        for k in range(TOP):
            ids_k = table[k : k + 1]
            rank_k = jnp.sum(jnp.where(expert == ids_k, rank, 0.0), axis=0, keepdims=True)
            ids_i = ids_k.astype(jnp.int32)
            place = (ids_i % NP) * CAP + rank_k.astype(jnp.int32)
            look[:, k * 128 : (k + 1) * 128] = jnp.where(lane_l == place, 1.0, 0.0).astype(BF16)
            zmask[:, k * 128 : (k + 1) * 128] = jnp.where(sub8 == ids_i // NP, 1.0, 0.0)

    def send_gates():
        @pl.loop(0, NP)
        def _(e):
            gm = nt(gate_g[...], pick[e])
            gm_s[e] = jnp.concatenate([gm, jnp.zeros((NP, 128 - ROWS), F32)], axis=1).astype(BF16)

        for i in range(1, NP):
            to = plane(i)
            remote(gm_s.at[to], gm_r.at[p], gm_ss, gm_rs, (z, to * 2 + core)).start()
        gm_r[p] = gm_s[p]

    def select(k):
        cols = pl.ds(STARTS[k], WIDTHS[k])
        w = WIDTHS[k]

        @pl.loop(0, NP // 4)
        def _(q):
            lhs = pick[pl.ds(q * 4, 4)].reshape(4 * ROWS, 1024)
            out = nn(lhs, tok[:, :, :, cols].reshape(1024, w))
            send[pl.ds(q * 4, 4), :, :, cols] = out.astype(BF16).reshape(4, CAP, SRC, w)

        for i in range(1, NP):
            to = plane(i)
            remote(
                send.at[to, :, :, cols], recv.at[:, p, :, cols], xy_s.at[k], xy_r.at[k],
                (z, to * 2 + core),
            ).start()
        recv[:, p, :, cols] = send[p, :, :, cols]

    r_i = iota((256, 256), 0)
    s_i = iota((256, 256), 1)
    perm = jnp.where(((r_i % 16) // 2) * 32 + (r_i // 16) * 2 + r_i % 2 == s_i, 1.0, 0.0).astype(BF16)
    back = jnp.where(((r_i % 32) // 2) * 16 + (r_i // 32) * 2 + r_i % 2 == s_i, 1.0, 0.0).astype(BF16)
    eye = jnp.where(r_i == s_i, 1.0, 0.0).astype(BF16)

    def hidden_task():
        h_in.wait()
        hx_cp.wait_recv()
        for j in range(2):
            for c in range(CAP):
                h_all[c, :, j * HALF_H : (j + 1) * HALF_H] = nn(perm, h_raw[j, c]).astype(BF16)

    def gate_task():
        wait_for(gm_r.at[pl.ds(0, NP - 1)], gm_rs)
        mine = jnp.where(iota((NP, NP, 128), 1) == p, gm_r[...].astype(F32), 0.0)
        gates = jnp.sum(mine, axis=1).astype(BF16)
        spread = jnp.where(iota((256, NP), 0) // SRC == iota((256, NP), 1), 1.0, 0.0).astype(BF16)
        wide = nn(spread, gates)
        lane = iota((256, 128), 1)
        src = iota((256, 128), 0) % SRC
        for c in range(CAP):
            col = jnp.sum(jnp.where(lane == c * SRC + src, wide, 0.0), axis=1, keepdims=True)
            gate_col[c] = jnp.broadcast_to(col, (256, 128))
            scaled = (col * h_all[c].astype(F32)).astype(BF16)
            for b in range(3):
                scaled_t[b * 256 : (b + 1) * 256, c * 256 : (c + 1) * 256] = nt(
                    eye, scaled[:, b * 256 : (b + 1) * 256]
                ).astype(BF16)

    def take_u(k):
        cols = pl.ds(STARTS[k], WIDTHS[k])
        w = WIDTHS[k]
        wait_for(recv.at[:, pl.ds(0, NP - 1), :, cols], xy_r.at[k])

        @pl.loop(0, CAP)
        def _(c):
            part = nt(recv[c, :, :, cols].reshape(256, w), w_v[:, cols])
            if k == 0:
                uacc[c] = part
            else:
                uacc[c] += part

    def take_w(k):
        cols = pl.ds(STARTS[k], WIDTHS[k])
        w = WIDTHS[k]

        @pl.loop(0, 3)
        def _(b):
            rows = pl.ds(pl.multiple_of(b * 256, 256), 256)
            out = nn(scaled_t[rows, :], recv[:, :, :, cols].reshape(5 * 256, w))
            dw_v[rows, cols] = out.astype(BF16)

        pltpu.make_async_copy(dw_v.at[:, cols], dw_hbm.at[:, cols], dw_sem.at[k]).start()

    def last_u(k):
        cols = pl.ds(STARTS[k], WIDTHS[k])
        w = WIDTHS[k]
        wait_for(recv.at[:, pl.ds(0, NP - 1), :, cols], xy_r.at[k])
        lane_t = iota((256, 128), 1)
        terms = jnp.zeros((256, 128), F32)
        for c in range(CAP):
            u = uacc[c] + nt(recv[c, :, :, cols].reshape(256, w), w_v[:, cols])
            uacc[c] = u
            exs[c].start()
            part = jnp.sum(u * h_all[c].astype(F32), axis=1, keepdims=True)
            terms = terms + jnp.where(lane_t == p * CAP + c, part, 0.0)
        gp_s[...] = terms.reshape(NP, SRC, 128)
        for i in range(1, NP):
            to = plane(i)
            remote(gp_s.at[to], gp_r.at[p], gp_ss, gp_rs, (z, to * 2 + core)).start()
        gp_r[p] = gp_s[p]

    exs = []
    for c in range(CAP):
        cp = remote(
            uacc.at[c, :, pl.ds(pl.multiple_of(other * HALF_H, 128), HALF_H)], uex.at[c],
            ex_s.at[c], ex_r.at[c], sibling,
        )
        exs.append(cp)

    for k in range(1, 4):
        hop23(k, 2)
    locals_[0].wait()
    swaps[0].wait_recv()
    wait_for(tok.at[pl.ds(0, NZ - 1), :, :, first_cols], first_r)
    select(0)
    hop23(1, 3)
    hop23(2, 3)
    send_gates()
    hop4(1)
    hidden_task()
    look_task()
    for t in range(1, K + 2):
        if t < K:
            gathered(t)
            select(t)
        if t + 1 < K:
            hop4(t + 1)
        if t + 2 < K:
            hop23(t + 2, 3)
        if t + 3 < K:
            hop23(t + 3, 2)
        if t + 4 < K:
            hop1(t + 4)
        if t == 1:
            gate_task()
            w_in.wait()
        if t >= 2 and t - 2 < K - 1:
            take_u(t - 2)
            take_w(t - 2)
    last_u(K - 1)
    take_w(K - 1)

    def finish_hidden(c):
        exs[c].wait_recv()
        u = uacc[c, :, pl.ds(pl.multiple_of(core * HALF_H, 128), HALF_H)] + uex[c]
        dh = (gate_col[c, :, 0:1] * u).astype(BF16)
        dh_v[c] = nn(back, dh).astype(BF16)
        pltpu.make_async_copy(dh_v.at[c], dh_hbm.at[c], dh_sem.at[c]).start()


    wait_for(gp_r.at[pl.ds(0, NP - 1)], gp_rs)
    total = jnp.sum(gp_r[...], axis=0)
    g2_s[...] = jnp.broadcast_to(total[:, None, :], (SRC, 8, 128))
    g2 = []
    for d in range(NZ):
        to = (z + d) % NZ
        for flip in (0, 1):
            if d == 0 and flip == 0:
                continue
            to_core = core if flip == 0 else other
            n = 2 * d + flip - 1
            cp = remote(
                g2_s.at[to * 2 + to_core], g2_r.at[core, z], g2_ss.at[n], g2_rs.at[n],
                (to, p * 2 + to_core),
            )
            cp.start()
            g2.append(cp)
    g2_r[core, z] = g2_s[z * 2 + core]
    for c in range(CAP):
        finish_hidden(c)
    for cp in g2:
        cp.wait_recv()
    summed = g2_r[0] + g2_r[1]
    zi = iota((NZ, 8, 128), 0)
    si = iota((NZ, 8, 128), 1)
    terms8 = jnp.sum(jnp.where(zi == si, summed, 0.0), axis=0)
    hi = terms8.astype(BF16)
    rest = terms8 - hi.astype(F32)
    mid = rest.astype(BF16)
    low = (rest - mid.astype(F32)).astype(BF16)
    got = nn(jnp.concatenate([hi, mid, low], axis=0), look[...])
    line_g = jnp.sum((got[0:8] + got[8:16] + got[16:24]) * zmask[...], axis=0, keepdims=True)
    for k in range(TOP):
        here = line_g[:, k * 128 : (k + 1) * 128]
        dgate_ref[k : k + 1, :] = jnp.where(core == 0, here[:, 0:TOK], here[:, TOK:])

    hx_cp.wait_send()
    for cp in swaps + idxs + exs + g2:
        cp.wait_send()
    for k in range(K):
        cols = pl.ds(STARTS[k], WIDTHS[k])
        wait_for(tok.at[pl.ds(0, NZ - 1), :, :, cols], z_s.at[k] if k else first_s)
        wait_for(recv.at[:, pl.ds(0, NP - 1), :, cols], xy_s.at[k])
        pltpu.make_async_copy(dw_v.at[:, cols], dw_hbm.at[:, cols], dw_sem.at[k]).wait()
    for c in range(CAP):
        pltpu.make_async_copy(dh_v.at[c], dh_hbm.at[c], dh_sem.at[c]).wait()
    wait_for(gm_r.at[pl.ds(0, NP - 1)], gm_ss)
    wait_for(gp_r.at[pl.ds(0, NP - 1)], gp_ss)


def copies(dg_in, dh_in, dw_in, dg_out, dh_out, dw_out, dg_v, dh_v, dw_v, sems):
    parts = []
    for i in range(8):
        rows = pl.ds(i * (H // 8), H // 8)
        parts.append((dw_in.at[rows], dw_v.at[rows], dw_out.at[rows]))
    for i in range(CAP):
        parts.append((dh_in.at[i], dh_v.at[i], dh_out.at[i]))
    parts.append((dg_in, dg_v, dg_out))
    loads = []
    for i, (src, mid, _) in enumerate(parts):
        cp = pltpu.make_async_copy(src, mid, sems.at[0, i])
        cp.start()
        loads.append(cp)
    stores = []
    for i, (_, mid, dst) in enumerate(parts):
        loads[i].wait()
        cp = pltpu.make_async_copy(mid, dst, sems.at[1, i])
        cp.start()
        stores.append(cp)
    for cp in stores:
        cp.wait()


def local(grad_out, expert_ids, gates, hidden_saved, w_down):
    dma = pltpu.SemaphoreType.DMA
    vm = pltpu.VMEM
    anywhere = pl.BlockSpec(memory_space=pl.ANY)
    in_vmem = pl.BlockSpec(memory_space=pltpu.VMEM)
    scratch = [
        vm((NZ, 2, TOK, HALF_D), BF16),
        vm((NP, CAP, SRC, HALF_D), BF16),
        vm((CAP, NP, SRC, HALF_D), BF16),
        vm((NP, ROWS, 1024), BF16),
        vm((H, HALF_D), BF16),
        vm((CAP, 256, H), F32),
        vm((2, CAP, 256, HALF_H), BF16),
        vm((CAP, 256, H), BF16),
        vm((H, CAP * 256), BF16),
        vm((H, HALF_D), BF16),
        vm((CAP, 256, HALF_H), F32),
        vm((CAP, 256, HALF_H), BF16),
        vm((CAP, 256, 128), F32),
        vm((16, 128), F32),
        vm((NZ, 2, 16, 128), F32),
        vm((NP, 1024), F32),
        vm((NP, 1024), BF16),
        vm((NP, NP, 128), BF16),
        vm((NP, NP, 128), BF16),
        vm((NP, SRC, 128), F32),
        vm((NP, SRC, 128), F32),
        vm((SRC, 8, 128), F32),
        vm((2, NZ, 8, 128), F32),
        vm((128, TOP * 128), BF16),
        vm((8, TOP * 128), F32),
        dma, dma, dma((K,)), dma((K,)), dma((K,)), dma((15,)), dma((15,)), dma((2,)), dma, dma,
        dma((K,)), dma((2, 4, K)), dma((K,)), dma((K,)), dma, dma, dma((CAP,)), dma((CAP,)),
        dma, dma, dma((15,)), dma((15,)), dma((K,)), dma((CAP,)),
    ]
    shapes = (
        jax.ShapeDtypeStruct((TOP, TOK), F32),
        jax.ShapeDtypeStruct((CAP, 256, HALF_H), BF16),
        jax.ShapeDtypeStruct((H, HALF_D), BF16),
    )
    results = pl.pallas_call(
        kernel,
        out_shape=shapes,
        in_specs=[anywhere, in_vmem, in_vmem, anywhere, anywhere],
        out_specs=(in_vmem, anywhere, anywhere),
        scratch_shapes=scratch,
        compiler_params=pltpu.CompilerParams(
            collective_id=0, has_side_effects=True, vmem_limit_bytes=56 * 2**20
        ),
        cost_estimate=pl.CostEstimate(
            flops=15 * 10**9, bytes_accessed=10 * 10**6, transcendentals=0
        ),
    )(grad_out, expert_ids.T, gates.T, jnp.transpose(hidden_saved[0], (1, 0, 2)), w_down[0])
    d_gate, d_hidden, d_weight = pl.pallas_call(
        copies,
        out_shape=shapes,
        in_specs=[anywhere] * 3,
        out_specs=(anywhere,) * 3,
        scratch_shapes=[
            vm((TOP, TOK), F32),
            vm((CAP, 256, HALF_H), BF16),
            vm((H, HALF_D), BF16),
            dma((2, 14)),
        ],
    )(*results)
    return d_gate.T, jnp.transpose(d_hidden, (1, 0, 2))[None], d_weight[None]


def solution(mesh):
    spec = P(("group", "fsdp"), None)
    in_specs = (
        spec,
        spec,
        spec,
        P(("group", "fsdp"), None, None, None),
        P(("group", "fsdp"), None, None),
    )
    out_specs = (spec, P(("group", "fsdp"), None, None, None), P(("group", "fsdp"), None, None))
    return jax.shard_map(local, mesh=mesh, in_specs=in_specs, out_specs=out_specs, check_vma=False)
```
